512 devices in a mesh: ax: 64 (over x, y_hi, z), circ: 8 (over y_lo, core).
Axes of the slice: x: 4, y: 8 (y_hi: 2, y_lo: 4; y = y_hi * 4 + y_lo), z: 8, core: 2. Of those that a mesh axis runs over, the one named last changes fastest.
Arguments:
- lam_start: bfloat16 [64, 42, 3072], P('ax', None, 'circ'), may hold values from -6 to 6
- rhs: bfloat16 [64, 42, 3072], P('ax', None, 'circ'), may hold values from -6 to 6
- state: bfloat16 [64, 42, 3072], P('ax', None, 'circ'), may hold values from -6 to 6
- blocks: bfloat16 [64, 96, 768], P('ax'), may hold values from -0.21875 to 0.21875
- slots: int32 [64, 8], P('ax'), may hold values from 0 to 8, as said below
- mass: float32 [64, 96], P('ax'), may hold values from 0.5 to 2
- precond: float32 [64, 96], P('ax'), may hold values from 0.2 to 0.6
- contact_blocks: bfloat16 [32768, 9216], P(('ax', 'circ')), may hold values from -0.625 to 0.625
- contact_flags: int32 [32768, 128], P(('ax', 'circ')), may hold values 0 or 1
- contact_owner: int32 [32768], P(('ax', 'circ')), may hold values from 0 to 63, as said below
- contact_row: int32 [32768], P(('ax', 'circ')), may hold values from 0 to 3
- contact_front: int32 [32768], P(('ax', 'circ')), may hold values from 0 to 1023
Outputs:
- adjoint: float32 [64, 42, 3072], P('ax', None, 'circ')
- sensitivity: float32 [1024], P('ax')
The draws below stay inside these ranges and needn't reach their ends.
Inputs may be any that keep to these rules, and one draw needn't show every extreme that they name: `slots`: each row lists 8 distinct codes, one of them 4; code c names the block at axial offset c // 3 - 1 and circumferential offset c mod 3 - 1. `contact_owner`: of the 64 contacts held by one device, at most 2 name any one section; for the devices that share a circ index, one section is named by exactly 2 contacts of every one of them.
All inputs are finite; a program needn't handle non-finite values. No bound on the sum of `contact_flags` on one device may be relied on, other than what follows from the above.
Results may differ from the reference program's by a relative error of at most 0.0032.
Values may be sent and summed in bfloat16 or wider, within the bound.
A program may use at most 64 MiB of HBM per device.

```python
import math
import jax
import jax.numpy as jnp
from jax import lax

BLK = 96
HARM = 42
SAMPLES = 128
NNZ = 8
RA = 1
RC = 4
CPD = 64
SEND = 2
SECTIONS = 64
SECTORS = 8
AXROWS = 64
CIRCOLS = 32
CONTACTS = 32768
FRONT = 1024


def draw_slots(key, part):
    row_keys = jax.random.split(key, AXROWS)

    def one_row(row_key):
        shuffled = jax.random.permutation(row_key, 9).astype(jnp.int32)
        slot_codes = shuffled[:NNZ]
        has_self = jnp.any(slot_codes == 4)
        position = jnp.arange(NNZ, dtype=jnp.int32)
        return jnp.where(jnp.logical_and(jnp.logical_not(has_self), position == NNZ - 1), 4, slot_codes).astype(jnp.int32)
    return jax.vmap(one_row)(row_keys)


def draw_contact_owner(key, part):
    crack_key, pick_key, order_key = jax.random.split(key, 3)
    crack_section = jax.random.randint(crack_key, (SECTORS,), 0, SECTIONS).astype(jnp.int32)
    devices = SECTIONS * SECTORS
    spread = SEND * (SECTIONS - 1)
    pick_keys = jax.random.split(pick_key, devices)
    order_keys = jax.random.split(order_key, devices)
    home_section = crack_section[jnp.arange(devices, dtype=jnp.int32) % SECTORS]

    def one_device(home, pick_one, order_one):
        offsets = jax.random.permutation(pick_one, spread)[:CPD - SEND].astype(jnp.int32)
        others = (home + 1 + offsets % (SECTIONS - 1)) % SECTIONS
        owners = jnp.concatenate([jnp.full((SEND,), home, dtype=jnp.int32), others.astype(jnp.int32)])
        return jax.random.permutation(order_one, owners)
    return jax.vmap(one_device)(home_section, pick_keys, order_keys).reshape(CONTACTS).astype(jnp.int32)


def plant(entries, own_key, least, largest):
    longest = entries.shape.index(max(entries.shape))
    spots = []
    for shift in (0, 1):
        where = [jax.random.randint(jax.random.fold_in(own_key, axis), (), 0, length) for axis, length in enumerate(entries.shape)]
        where[longest] = (where[longest] + shift) % entries.shape[longest]
        spots.append(tuple(where))
    return entries.at[spots[0]].set(least).at[spots[1]].set(largest)


def levels(key, dims, cuts, smallest, top_value):
    factor_of, own = 1.0, jax.random.fold_in(key, 6)
    for dim, blocks in cuts:
        steps = jnp.exp(jax.random.uniform(jax.random.fold_in(own, dim), (blocks,), jnp.float32, smallest / len(cuts), top_value / len(cuts)))
        factor_of = factor_of * jnp.repeat(steps, dims[dim] // blocks).reshape([-1 if axis == dim else 1 for axis in range(len(dims))])
    return factor_of


def noise(stream_key, shape, scale, limit, cuts=(), kind=jnp.bfloat16):
    entries = scale * jax.random.normal(stream_key, shape, jnp.float32)
    if cuts:
        entries = entries * levels(stream_key, shape, cuts, -0.22, 0.18)
    return jnp.clip(entries, -limit, limit).astype(kind)


def setup_inputs(seed: int = 0) -> dict:
    streams_of = jax.random.split(jax.random.key(seed), 13)
    lam_start = noise(streams_of[0], (AXROWS, HARM, CIRCOLS * BLK), 1.0, 6.0, ((0, 64), (2, 8)))
    rhs = noise(streams_of[1], (AXROWS, HARM, CIRCOLS * BLK), 1.0, 6.0, ((0, 64), (2, 8)))
    state = noise(streams_of[2], (AXROWS, HARM, CIRCOLS * BLK), 1.0, 6.0, ((0, 64), (2, 8)))
    blocks = noise(streams_of[3], (AXROWS, BLK, NNZ * BLK), (NNZ * BLK) ** -0.5, 0.21875, ((0, 64),))
    slots = draw_slots(jax.random.fold_in(streams_of[12], 71), 0)
    mass = jnp.clip(jnp.exp(math.log(2.0) - 1.3862944 * jax.random.uniform(streams_of[5], (AXROWS, BLK), jnp.float32) ** levels(streams_of[5], (AXROWS, BLK), ((0, 64),), -0.2, 0.2)), 0.5, 2.0)
    precond = jnp.clip(jnp.exp(math.log(0.6) - 1.0986123 * jax.random.uniform(streams_of[6], (AXROWS, BLK), jnp.float32) ** levels(streams_of[6], (AXROWS, BLK), ((0, 64),), -0.2, 0.2)), 0.2, 0.6)
    contact_blocks = noise(streams_of[7], (CONTACTS, BLK * BLK), BLK ** -0.5, 0.625, ((0, 512),))
    contact_flags = plant((jax.random.randint(streams_of[8], (CONTACTS, SAMPLES), 0, 2) < 1).astype(jnp.int32), jax.random.fold_in(streams_of[8], 1), 0, 1)
    contact_owner = draw_contact_owner(jax.random.fold_in(streams_of[12], 71), 0)
    contact_row = plant(jax.random.randint(streams_of[10], (CONTACTS,), 0, RA * RC), jax.random.fold_in(streams_of[10], 1), 0, (RA * RC) - 1).astype(jnp.int32)
    contact_front = plant(jax.random.randint(streams_of[11], (CONTACTS,), 0, FRONT), jax.random.fold_in(streams_of[11], 1), 0, FRONT - 1).astype(jnp.int32)
    return dict(lam_start=lam_start, rhs=rhs, state=state, blocks=blocks, slots=slots, mass=mass, precond=precond, contact_blocks=contact_blocks, contact_flags=contact_flags, contact_owner=contact_owner, contact_row=contact_row, contact_front=contact_front)


omega_rate = 0.05
sens_scale = 0.015625


def time_table(samples, columns):
    moments = jnp.arange(samples).astype(jnp.float32)[:, None]
    column_ids = jnp.arange(columns, dtype=jnp.int32)[None, :]
    orders = (column_ids // 2 + 1).astype(jnp.float32)
    phases = (2.0 * math.pi / samples) * moments * orders
    return jnp.where(column_ids % 2 == 0, jnp.cos(phases), jnp.sin(phases))


def harmonic_filters(flag_rows, time_rows):
    weighted = flag_rows.astype(jnp.float32)[:, :, None] * time_rows[None, :, :]
    return (2.0 / time_rows.shape[0]) * jnp.einsum('kth,tg->khg', weighted, time_rows, precision=lax.Precision.HIGHEST)


def mass_factors(columns):
    orders = (jnp.arange(columns, dtype=jnp.int32) // 2 + 1).astype(jnp.float32)
    return (omega_rate * orders) ** 2


def pick_rows(field_rows, wanted, sector_cols):
    shaped = field_rows.reshape(field_rows.shape[0], field_rows.shape[1], sector_cols, -1)
    chosen = shaped[wanted // sector_cols, :, wanted % sector_cols, :]
    return jnp.transpose(chosen, (1, 0, 2))


def add_rows(accumulated, wanted, values, sector_cols):
    shaped = accumulated.reshape(accumulated.shape[0], accumulated.shape[1], sector_cols, -1)
    shaped = shaped.at[wanted // sector_cols, :, wanted % sector_cols, :].add(jnp.transpose(values, (1, 0, 2)))
    return shaped.reshape(accumulated.shape)


def adjoint_effect(picked, blocks_flat, filters):
    square = blocks_flat.reshape(blocks_flat.shape[0], BLK, BLK).astype(jnp.float32)
    coupled = jnp.einsum('gkq,kqp->gkp', picked.astype(jnp.float32), square, precision=lax.Precision.HIGHEST)
    return jnp.einsum('khg,gkp->hkp', filters, coupled, precision=lax.Precision.HIGHEST)


def forward_effect(picked, blocks_flat, filters):
    square = blocks_flat.reshape(blocks_flat.shape[0], BLK, BLK).astype(jnp.float32)
    coupled = jnp.einsum('gkq,kpq->gkp', picked.astype(jnp.float32), square, precision=lax.Precision.HIGHEST)
    return jnp.einsum('khg,gkp->hkp', filters, coupled, precision=lax.Precision.HIGHEST)


def stiffness_apply(lowered, blocks, slots):
    shaped = lowered.reshape(AXROWS, HARM, CIRCOLS, BLK)
    wrapped = jnp.concatenate([shaped[:, :, -1:], shaped, shaped[:, :, :1]], axis=2)
    border = jnp.zeros((1, HARM, CIRCOLS + 2, BLK), lowered.dtype)
    extended = jnp.concatenate([border, wrapped, border], axis=0)
    zero_index = jnp.zeros((), jnp.int32)

    def one_row(position):
        slot_codes = slots[position].astype(jnp.int32)
        pieces = []
        for slot_index in range(NNZ):
            slot_code = slot_codes[slot_index]
            start_row = (position + slot_code // 3).astype(jnp.int32)
            start_col = (slot_code % 3).astype(jnp.int32)
            block_slice = lax.dynamic_slice(extended, (start_row, zero_index, start_col, zero_index), (1, HARM, CIRCOLS, BLK))
            pieces.append(block_slice[0])
        stacked = jnp.stack(pieces, axis=2).reshape(HARM * CIRCOLS, NNZ * BLK)
        product = lax.dot_general(stacked, blocks[position], (((1,), (1,)), ((), ())), preferred_element_type=jnp.float32)
        return product.reshape(HARM, CIRCOLS * BLK)

    return lax.map(one_row, jnp.arange(AXROWS, dtype=jnp.int32))


def reference(lam_start, rhs, state, blocks, slots, mass, precond, contact_blocks, contact_flags, contact_owner, contact_row, contact_front):
    time_rows = time_table(SAMPLES, HARM)
    filters = harmonic_filters(contact_flags, time_rows)
    factors = mass_factors(HARM)
    mass_term = factors[None, :, None] * jnp.tile(mass, (1, CIRCOLS))[:, None, :]
    relaxation = jnp.tile(precond, (1, CIRCOLS))[:, None, :]
    rhs_full = rhs.astype(jnp.float32)
    holder = jnp.arange(CONTACTS, dtype=jnp.int32) // CPD
    target_sector = holder % SECTORS
    target_rows = (contact_owner * RA + contact_row // RC) * CIRCOLS + target_sector * RC + contact_row % RC

    def relax_sweep(current):
        lowered = current.astype(jnp.bfloat16)
        picked = pick_rows(lowered, target_rows, CIRCOLS)
        effect = adjoint_effect(picked, contact_blocks, filters)
        contact_sum = add_rows(jnp.zeros(current.shape, jnp.float32), target_rows, effect, CIRCOLS)
        applied = stiffness_apply(lowered, blocks, slots) - mass_term * current + contact_sum
        return current + relaxation * (rhs_full - applied)

    halfway = relax_sweep(lam_start.astype(jnp.float32))
    adjoint = relax_sweep(halfway)
    adjoint_low = adjoint.astype(jnp.bfloat16)
    picked_state = pick_rows(state, target_rows, CIRCOLS)
    picked_adjoint = pick_rows(adjoint_low, target_rows, CIRCOLS)
    effect = forward_effect(picked_state, contact_blocks, filters)
    front_parts = -sens_scale * jnp.sum(picked_adjoint.astype(jnp.float32) * effect, axis=(0, 2))
    sensitivity = jnp.zeros((FRONT,), jnp.float32).at[contact_front].add(front_parts)
    return adjoint, sensitivity
```

```python
import math

import jax
import jax.numpy as jnp
import numpy as np
from jax import lax
from jax.experimental import pallas as pl
from jax.experimental.pallas import tpu as pltpu
from jax.sharding import PartitionSpec as P

BLK = 96
HARM = 42
SAMPLES = 128
NNZ = 8
RC = 4
CPD = 64
SECTIONS = 64
SECTORS = 8
SLOTS = 2 * SECTIONS
STEP = 29
GROUP = 4

omega_rate = 0.05
sens_scale = 0.015625

F32 = jnp.float32
BF16 = jnp.bfloat16
HIGHEST = lax.Precision.HIGHEST
MESH = pl.DeviceIdType.MESH


def time_table():
    moments = np.arange(SAMPLES)[:, None]
    columns = np.arange(48)[None, :]
    phases = (2.0 * math.pi / SAMPLES) * ((moments * (columns // 2 + 1)) % SAMPLES)
    rows = np.where(columns % 2 == 0, np.cos(phases), np.sin(phases))
    rows[:, HARM:] = 0.0
    return rows.T.astype(np.float32)


def iota(shape, dim):
    return lax.broadcasted_iota(jnp.int32, shape, dim)


def dot(a, b, dims, precision=None):
    return lax.dot_general(a, b, (dims, ((), ())), precision=precision, preferred_element_type=F32)


NT = ((1,), (1,))
NN = ((1,), (0,))


def kernel(
    lam_ref, rhs_ref, state_ref, blocks_ref, slots_ref, mass_ref, precond_ref, contacts_ref,
    flags_ref, owner_ref, row_ref, front_ref, table_ref,
    adj_ref, sens_ref,
    idx_v, idx_s, meta_out, meta_in, send_buf, recv_buf, unpack, turned, chosen, acc, codes, fronts,
    onehot_lo, onehot_hi, rhs_buf, cur, base, ext1, ext2, wide, state_pad, xw, yw, bw, sums,
    part_a, recv_a, part_b, recv_b, part_c, recv_c,
    local_sem, meta_send, meta_recv, block_send, block_recv, halo_send, halo_recv,
    a_send, a_recv, b_send, b_recv, c_send, c_recv,
):
    ax = lax.axis_index("ax")
    ci = lax.axis_index("circ")
    xy, zz = ax // 8, lax.rem(ax, 8)

    def offset(i):
        return lax.rem(i * STEP, SECTIONS)

    def ax_peer(i):
        return lax.rem(ax + offset(i), SECTIONS)

    def around(da, dc):
        return (lax.rem(ax + da + SECTIONS, SECTIONS), lax.rem(ci + dc + SECTORS, SECTORS))

    corners = [(1, 1), (1, -1), (-1, 1), (-1, -1)]
    barrier = pltpu.get_barrier_semaphore()

    def greet(i, carry):
        pl.semaphore_signal(barrier, inc=1, device_id=(ax_peer(i), ci), device_id_type=MESH)
        return carry

    lax.fori_loop(1, SECTIONS, greet, 0)

    def greet_circ(j, carry):
        pl.semaphore_signal(barrier, inc=1, device_id=(ax, lax.rem(ci + j, SECTORS)), device_id_type=MESH)
        return carry

    lax.fori_loop(1, SECTORS, greet_circ, 0)
    for da, dc in corners:
        pl.semaphore_signal(barrier, inc=1, device_id=around(da, dc), device_id_type=MESH)

    eye64 = (iota((CPD, CPD), 0) == iota((CPD, CPD), 1)).astype(jnp.int32)

    def column(row):
        return jnp.sum(eye64 * row, axis=1, keepdims=True)

    owner_row = owner_ref[...]
    owner_col = column(owner_row)
    row_col = column(row_ref[...])
    front_col = column(front_ref[...])
    same = (owner_col == owner_row).astype(jnp.int32)
    below = (iota((CPD, CPD), 0) < iota((CPD, CPD), 1)).astype(jnp.int32)
    above = (iota((CPD, CPD), 1) < iota((CPD, CPD), 0)).astype(jnp.int32)
    dest_row = 2 * owner_row + jnp.sum(same * below, axis=0, keepdims=True)
    dest_col = 2 * owner_col + jnp.sum(same * above, axis=1, keepdims=True)
    hit = (dest_col == iota((CPD, SLOTS), 1)).astype(jnp.int32)
    index_row = jnp.sum(hit * iota((CPD, SLOTS), 0), axis=0, keepdims=True)
    idx_v[...] = jnp.broadcast_to(index_row, (8, SLOTS))
    to_scalar = pltpu.make_async_copy(idx_v, idx_s, local_sem.at[0])
    to_scalar.start()

    line = iota((8 * SECTIONS, CPD), 0)
    slot_of_line = 2 * (line // 8) + lax.rem(line, 2)
    kind_of_line = lax.rem(line, 8) // 2
    picks = dest_row == slot_of_line
    pick_codes = (picks & (kind_of_line == 0)).astype(BF16)
    pick_fronts = (picks & (kind_of_line == 1)).astype(BF16)
    coded = (flags_ref[...] * (row_col + 1)).astype(F32).astype(BF16)
    numbered = jnp.where(iota((CPD, 128), 1) < 64, front_col // 32, lax.rem(front_col, 32)).astype(F32).astype(BF16)
    meta = dot(pick_codes, coded, NN) + dot(pick_fronts, numbered, NN)
    meta_out[...] = meta.reshape(SECTIONS, 8, 128).astype(BF16)

    def pad_rows(ref, source):
        ref[...] = jnp.zeros(ref.shape, ref.dtype)
        for r in range(RC):
            ref[r, 0:HARM, 0:BLK] = source[0, :, r * BLK : (r + 1) * BLK].astype(F32)

    pad_rows(cur, lam_ref)
    ext1[1, 1:5] = cur[...].astype(BF16)

    pl.semaphore_wait(barrier, SECTIONS - 1 + SECTORS - 1 + len(corners))

    def halo(ext, sweep):
        moves = [
            (ext.at[1, 1:5], ext.at[0, 1:5], (1, 0)),
            (ext.at[1, 1:5], ext.at[2, 1:5], (-1, 0)),
            (ext.at[1, 4], ext.at[1, 0], (0, 1)),
            (ext.at[1, 1], ext.at[1, 5], (0, -1)),
            (ext.at[1, 4], ext.at[0, 0], (1, 1)),
            (ext.at[1, 1], ext.at[0, 5], (1, -1)),
            (ext.at[1, 4], ext.at[2, 0], (-1, 1)),
            (ext.at[1, 1], ext.at[2, 5], (-1, -1)),
        ]
        return [
            pltpu.make_async_remote_copy(
                src_ref=source, dst_ref=target, send_sem=halo_send.at[sweep, n], recv_sem=halo_recv.at[sweep, n],
                device_id=around(*way), device_id_type=MESH,
            )
            for n, (source, target, way) in enumerate(moves)
        ]

    halo1 = halo(ext1, 0)
    for copy in halo1:
        copy.start()

    def meta_copy(i):
        return pltpu.make_async_remote_copy(
            src_ref=meta_out.at[ax_peer(i)], dst_ref=meta_in.at[i], send_sem=meta_send.at[i],
            recv_sem=meta_recv.at[i], device_id=(ax_peer(i), ci), device_id_type=MESH,
        )

    def block_copy(i):
        return pltpu.make_async_remote_copy(
            src_ref=send_buf.at[i], dst_ref=recv_buf.at[i], send_sem=block_send.at[i],
            recv_sem=block_recv.at[i], device_id=(ax_peer(i), ci), device_id_type=MESH,
        )

    def start_meta(i, carry):
        meta_copy(i).start()
        return carry

    to_scalar.wait()

    def start_block(i, carry):
        slot = 2 * ax_peer(i)
        send_buf[i, 0:24, :] = contacts_ref[idx_s[0, slot]]
        send_buf[i, 24:48, :] = contacts_ref[idx_s[0, slot + 1]]
        block_copy(i).start()
        return carry

    lax.fori_loop(1, 9, start_block, 0)
    lax.fori_loop(1, SECTIONS, start_meta, 0)
    lax.fori_loop(9, SECTIONS, start_block, 0)
    recv_buf[0, 0:24, :] = contacts_ref[idx_s[0, 2 * ax]]
    recv_buf[0, 24:48, :] = contacts_ref[idx_s[0, 2 * ax + 1]]
    meta_in[0] = meta_out[ax]

    spot = iota((128, 128), 0)
    mixed = (iota((128, 128), 1) == 4 * lax.rem(spot, 24) + spot // 24) & (spot < BLK)
    mixer = mixed.astype(BF16)
    plain = (iota((128, 128), 1) == spot).astype(BF16)
    table = table_ref[...]
    table_hi = table.astype(BF16)
    table_lo = (table - table_hi.astype(F32)).astype(BF16)

    def spread(rows, order):
        turn = dot(order, rows, NT).astype(BF16)
        return dot(turn, table_hi, NN) + dot(turn, table_lo, NN)

    pad_rows(state_pad, state_ref)
    for r in range(RC):
        lanes = slice(r * SAMPLES, (r + 1) * SAMPLES)
        xw[:, lanes] = spread(ext1[1, 1 + r], mixer).astype(BF16)
        yw[:, lanes] = spread(state_pad[r].astype(BF16), plain).astype(BF16)
    pad_rows(rhs_buf, rhs_ref)
    wide[...] = jnp.zeros(wide.shape, F32)
    for s in range(NNZ):
        wide[s, :, 0:BLK] = blocks_ref[0, :, s * BLK : (s + 1) * BLK].astype(F32)
    acc[...] = jnp.zeros(acc.shape, F32)
    unpack[...] = jnp.zeros(unpack.shape, F32)

    def wait_meta(i, carry):
        meta_copy(i).wait_recv()
        return carry

    lax.fori_loop(1, SECTIONS, wait_meta, 0)

    def spread_meta(i, carry):
        rows = meta_in[i].astype(F32)
        codes[pl.ds(2 * i, 2), :] = rows[0:2]
        fronts[pl.ds(2 * i, 2), :] = rows[2:4]
        return carry

    lax.fori_loop(0, SECTIONS, spread_meta, 0)
    eye128 = (spot == iota((128, 128), 1)).astype(F32)
    high, low = fronts[:, 0:1], fronts[:, 64:65]
    major = jnp.floor(high * 0.25)
    minor = (high - 4.0 * major) * 32.0 + low
    onehot_lo[...] = (minor == iota((128, 128), 1).astype(F32)).astype(F32)
    major_row = jnp.sum(eye128 * major, axis=0, keepdims=True)
    onehot_hi[...] = (major_row == iota((8, 128), 0).astype(F32)).astype(F32)

    precond = precond_ref[...]
    harmonic = (iota((48, BLK), 0) // 2 + 1).astype(F32) * omega_rate
    mass_term = harmonic * harmonic * mass_ref[...]

    def stiffness(ext):
        total = jnp.zeros((RC * 48, BLK), F32)
        for s in range(NNZ):
            code = slots_ref[0, s]
            rows = ext[code // 3, pl.ds(lax.rem(code, 3), RC)].reshape(RC * 48, 128)
            total = total + dot(rows, wide[s].astype(BF16), NT)
        return total

    def finish_halo(ext, copies):
        for copy in copies:
            copy.wait_recv()

        @pl.when(ax == 0)
        def _():
            ext[0] = jnp.zeros(ext.shape[1:], BF16)

        @pl.when(ax == SECTIONS - 1)
        def _():
            ext[2] = jnp.zeros(ext.shape[1:], BF16)

    def smooth(ext):
        total = stiffness(ext)
        for r in range(RC):
            now = cur[r, :, 0:BLK]
            applied = total[r * 48 : (r + 1) * 48] - mass_term * now
            base[r, :, 0:BLK] = now + precond * (rhs_buf[r, :, 0:BLK] - applied)

    finish_halo(ext1, halo1)
    base[...] = jnp.zeros(base.shape, F32)
    smooth(ext1)

    def masks(k):
        code = codes[pl.ds(k, 1), :]
        return [(code == float(r + 1)).astype(F32) for r in range(RC)]

    def take(i):
        for j in range(2):
            k = 2 * i + j
            for c in range(4):
                unpack[j, 24 * c : 24 * c + 24, 0:BLK] = recv_buf[i, 24 * j : 24 * j + 24, c * BLK : (c + 1) * BLK].astype(F32)
            square = unpack[j]
            flat = square[0:BLK].astype(BF16)
            turn = square.T[0:BLK].astype(BF16)
            turned[k] = turn
            mask = masks(k)
            forward = dot(flat, yw[...], NN)
            backward = dot(turn, xw[...], NN)
            kept = jnp.zeros((BLK, SAMPLES), F32)
            for r in range(RC):
                lanes = slice(r * SAMPLES, (r + 1) * SAMPLES)
                kept = kept + forward[:, lanes] * mask[r]
                acc[:, lanes] += backward[:, lanes] * mask[r]
            chosen[k] = kept

    take(0)

    def take_next(i, carry):
        block_copy(i).wait_recv()
        take(i)
        return carry

    lax.fori_loop(1, SECTIONS, take_next, 0)

    def settle(r):
        lanes = slice(r * SAMPLES, (r + 1) * SAMPLES)
        effect = dot(table, acc[:, lanes], NT, HIGHEST) * (2.0 / SAMPLES)
        return base[r, :, 0:BLK] - precond * effect

    for r in range(RC):
        cur[r, :, 0:BLK] = settle(r)
    ext2[1, 1:5] = cur[...].astype(BF16)
    halo2 = halo(ext2, 1)
    for copy in halo2:
        copy.start()
    for r in range(RC):
        lanes = slice(r * SAMPLES, (r + 1) * SAMPLES)
        xw[:, lanes] = spread(ext2[1, 1 + r], mixer).astype(BF16)

    acc[...] = jnp.zeros(acc.shape, F32)

    def again(g, carry):
        k = g * GROUP
        lhs = turned[pl.ds(k, GROUP)].reshape(GROUP * BLK, 128)
        product = dot(lhs, xw[...], NN)
        for j in range(GROUP):
            mask = masks(k + j)
            for r in range(RC):
                lanes = slice(r * SAMPLES, (r + 1) * SAMPLES)
                acc[:, lanes] += product[j * BLK : (j + 1) * BLK, lanes] * mask[r]
        return carry

    lax.fori_loop(0, SLOTS // GROUP, again, 0)
    finish_halo(ext2, halo2)
    smooth(ext2)
    for r in range(RC):
        final = settle(r)
        adj_ref[0, :, r * BLK : (r + 1) * BLK] = final[0:HARM]
        cur[r, :, 0:BLK] = final
    for r in range(RC):
        bw[r] = spread(cur[r].astype(BF16), mixer)[0:BLK]

    def part(k, carry):
        mask = masks(k)
        weight = bw[0] * mask[0]
        for r in range(1, RC):
            weight = weight + bw[r] * mask[r]
        sums[pl.ds(k, 1), :] = jnp.sum(chosen[k] * weight, axis=0, keepdims=True)
        return carry

    lax.fori_loop(0, SLOTS, part, 0)
    parts = jnp.sum(sums[...], axis=1, keepdims=True) * (-sens_scale * 2.0 / SAMPLES)
    own = dot(onehot_hi[...], onehot_lo[...] * parts, NN, HIGHEST)

    def everyone(peers, me, out_of, into, send, recv):
        def copies(j):
            there = lax.rem(me + j, 8)
            going = pltpu.make_async_remote_copy(
                src_ref=out_of(there), dst_ref=into.at[me], send_sem=send.at[j], recv_sem=recv.at[me],
                device_id=peers(there), device_id_type=MESH,
            )
            coming = pltpu.make_async_remote_copy(
                src_ref=out_of(there), dst_ref=into.at[there], send_sem=send.at[j], recv_sem=recv.at[there],
                device_id=peers(there), device_id_type=MESH,
            )
            return going, coming

        pairs = [copies(j) for j in range(1, 8)]
        for going, _ in pairs:
            going.start()
        for _, coming in pairs:
            coming.wait_recv()
        total = into[0]
        for n in range(1, 8):
            total = total + into[n]
        return total, [going for going, _ in pairs]

    part_a[...] = own
    recv_a[ci] = own
    total, sent_a = everyone(lambda j: (ax, j), ci, lambda j: part_a, recv_a, a_send, a_recv)
    for n in range(8):
        part_b[n] = total[n : n + 1]
    recv_b[xy] = part_b[xy]
    total, sent_b = everyone(lambda j: (j * 8 + zz, ci), xy, lambda j: part_b.at[j], recv_b, b_send, b_recv)
    part_c[...] = total
    recv_c[zz] = total
    total, sent_c = everyone(lambda j: (xy * 8 + j, ci), zz, lambda j: part_c, recv_c, c_send, c_recv)
    sens_ref[...] = pltpu.roll(jnp.broadcast_to(total, (8, 128)), lax.rem(128 - 16 * zz, 128), 1)

    for copy in halo1 + halo2 + sent_a + sent_b + sent_c:
        copy.wait_send()

    def drain(i, carry):
        meta_copy(i).wait_send()
        block_copy(i).wait_send()
        return carry

    lax.fori_loop(1, SECTIONS, drain, 0)


def shards(
    lam_start, rhs, state, blocks, slots, mass, precond, contact_blocks, contact_flags,
    contact_owner, contact_row, contact_front,
):
    packed = contact_blocks.reshape(CPD, 24, 384)
    table = jnp.asarray(time_table())
    vmem = pl.BlockSpec(memory_space=pltpu.VMEM)
    smem = pl.BlockSpec(memory_space=pltpu.SMEM)
    dma = pltpu.SemaphoreType.DMA
    scratch = [
        pltpu.VMEM((8, SLOTS), jnp.int32),
        pltpu.SMEM((8, SLOTS), jnp.int32),
        pltpu.VMEM((SECTIONS, 8, 128), BF16),
        pltpu.VMEM((SECTIONS, 8, 128), BF16),
        pltpu.VMEM((SECTIONS, 48, 384), BF16),
        pltpu.VMEM((SECTIONS, 48, 384), BF16),
        pltpu.VMEM((2, 128, 128), F32),
        pltpu.VMEM((SLOTS, BLK, 128), BF16),
        pltpu.VMEM((SLOTS, BLK, SAMPLES), F32),
        pltpu.VMEM((BLK, RC * SAMPLES), F32),
        pltpu.VMEM((SLOTS, 128), F32),
        pltpu.VMEM((SLOTS, 128), F32),
        pltpu.VMEM((SLOTS, 128), F32),
        pltpu.VMEM((8, SLOTS), F32),
        pltpu.VMEM((RC, 48, 128), F32),
        pltpu.VMEM((RC, 48, 128), F32),
        pltpu.VMEM((RC, 48, 128), F32),
        pltpu.VMEM((3, 6, 48, 128), BF16),
        pltpu.VMEM((3, 6, 48, 128), BF16),
        pltpu.VMEM((NNZ, BLK, 128), F32),
        pltpu.VMEM((RC, 48, 128), F32),
        pltpu.VMEM((128, RC * SAMPLES), BF16),
        pltpu.VMEM((128, RC * SAMPLES), BF16),
        pltpu.VMEM((RC, BLK, SAMPLES), F32),
        pltpu.VMEM((SLOTS, 128), F32),
        pltpu.VMEM((8, 128), F32),
        pltpu.VMEM((8, 8, 128), F32),
        pltpu.VMEM((8, 1, 128), F32),
        pltpu.VMEM((8, 1, 128), F32),
        pltpu.VMEM((1, 128), F32),
        pltpu.VMEM((8, 1, 128), F32),
        dma((1,)), dma((SECTIONS,)), dma((SECTIONS,)), dma((SECTIONS,)), dma((SECTIONS,)),
        dma((2, 8)), dma((2, 8)), dma((8,)), dma((8,)), dma((8,)), dma((8,)), dma((8,)), dma((8,)),
    ]
    adjoint, sums = pl.pallas_call(
        kernel,
        out_shape=(
            jax.ShapeDtypeStruct((1, HARM, RC * BLK), F32),
            jax.ShapeDtypeStruct((8, 128), F32),
        ),
        in_specs=[vmem, vmem, vmem, vmem, smem] + [vmem] * 8,
        out_specs=(vmem, vmem),
        scratch_shapes=scratch,
        compiler_params=pltpu.CompilerParams(
            collective_id=0, has_side_effects=True, vmem_limit_bytes=56 * 2**20
        ),
        cost_estimate=pl.CostEstimate(flops=4 * 10**9, bytes_accessed=3 * 10**6, transcendentals=0),
    )(
        lam_start, rhs, state, blocks, slots, mass, precond, packed, contact_flags,
        contact_owner.reshape(1, CPD), contact_row.reshape(1, CPD), contact_front.reshape(1, CPD), table,
    )
    return adjoint, sums[0, :16]


def solution(mesh):
    in_specs = (
        P("ax", None, "circ"),
        P("ax", None, "circ"),
        P("ax", None, "circ"),
        P("ax", None, None),
        P("ax", None),
        P("ax", None),
        P("ax", None),
        P(("ax", "circ"), None),
        P(("ax", "circ"), None),
        P(("ax", "circ")),
        P(("ax", "circ")),
        P(("ax", "circ")),
    )
    out_specs = (P("ax", None, "circ"), P("ax"))
    return jax.shard_map(shards, mesh=mesh, in_specs=in_specs, out_specs=out_specs, check_vma=False)
```

```python
import math

import jax
import jax.numpy as jnp
import numpy as np
from jax import lax
from jax.experimental import pallas as pl
from jax.experimental.pallas import tpu as pltpu
from jax.sharding import PartitionSpec as P

BLK = 96
HARM = 42
SAMPLES = 128
NNZ = 8
RC = 4
CPD = 64
SECTIONS = 64
SECTORS = 8
SLOTS = 2 * SECTIONS
STEP = 29
GROUP = 8
WINDOW = 16
LEN = 72
MSG = 2 * LEN + 8

omega_rate = 0.05
sens_scale = 0.015625

F32 = jnp.float32
BF16 = jnp.bfloat16
HIGHEST = lax.Precision.HIGHEST
MESH = pl.DeviceIdType.MESH


def time_table():
    moments = np.arange(SAMPLES)[:, None]
    columns = np.arange(48)[None, :]
    phases = (2.0 * math.pi / SAMPLES) * ((moments * (columns // 2 + 1)) % SAMPLES)
    rows = np.where(columns % 2 == 0, np.cos(phases), np.sin(phases))
    rows[:, HARM:] = 0.0
    return rows.T.astype(np.float32)


def iota(shape, dim):
    return lax.broadcasted_iota(jnp.int32, shape, dim)


def dot(a, b, dims, precision=None):
    return lax.dot_general(a, b, (dims, ((), ())), precision=precision, preferred_element_type=F32)


NT = ((1,), (1,))
NN = ((1,), (0,))


def kernel(
    lam_ref, rhs_ref, state_ref, blocks_ref, slots_ref, mass_ref, precond_ref, contacts_ref,
    flags_ref, owner_ref, row_ref, front_ref, table_ref,
    adj_ref, sens_ref,
    idx_v, idx_s, meta_out, send_buf, recv_buf, unpack, turned, chosen, acc, codes, fronts,
    onehot_lo, onehot_hi, rhs_buf, cur, base, ext1, ext2, wide, state_pad, xw, yw, bw, sums,
    part_a, recv_a, part_b, recv_b, part_c, recv_c,
    local_sem, block_send, block_recv, halo_send, halo_recv,
    a_send, a_recv, b_send, b_recv, c_send, c_recv,
):
    ax = lax.axis_index("ax")
    ci = lax.axis_index("circ")
    xy, zz = ax // 8, lax.rem(ax, 8)

    def offset(i):
        return lax.rem(i * STEP, SECTIONS)

    def ax_peer(i):
        return lax.rem(ax + offset(i), SECTIONS)

    def around(da, dc):
        return (lax.rem(ax + da + SECTIONS, SECTIONS), lax.rem(ci + dc + SECTORS, SECTORS))

    corners = [(1, 1), (1, -1), (-1, 1), (-1, -1)]
    barrier = pltpu.get_barrier_semaphore()

    def greet(i, carry):
        pl.semaphore_signal(barrier, inc=1, device_id=(ax_peer(i), ci), device_id_type=MESH)
        return carry

    lax.fori_loop(1, SECTIONS, greet, 0)

    def greet_circ(j, carry):
        pl.semaphore_signal(barrier, inc=1, device_id=(ax, lax.rem(ci + j, SECTORS)), device_id_type=MESH)
        return carry

    lax.fori_loop(1, SECTORS, greet_circ, 0)
    for da, dc in corners:
        pl.semaphore_signal(barrier, inc=1, device_id=around(da, dc), device_id_type=MESH)

    eye64 = (iota((CPD, CPD), 0) == iota((CPD, CPD), 1)).astype(jnp.int32)

    def column(row):
        return jnp.sum(eye64 * row, axis=1, keepdims=True)

    owner_row = owner_ref[...]
    owner_col = column(owner_row)
    row_col = column(row_ref[...])
    front_col = column(front_ref[...])
    same = (owner_col == owner_row).astype(jnp.int32)
    below = (iota((CPD, CPD), 0) < iota((CPD, CPD), 1)).astype(jnp.int32)
    above = (iota((CPD, CPD), 1) < iota((CPD, CPD), 0)).astype(jnp.int32)
    dest_row = 2 * owner_row + jnp.sum(same * below, axis=0, keepdims=True)
    dest_col = 2 * owner_col + jnp.sum(same * above, axis=1, keepdims=True)
    hit = (dest_col == iota((CPD, SLOTS), 1)).astype(jnp.int32)
    index_row = jnp.sum(hit * iota((CPD, SLOTS), 0), axis=0, keepdims=True)
    idx_v[...] = jnp.broadcast_to(index_row, (8, SLOTS))
    to_scalar = pltpu.make_async_copy(idx_v, idx_s, local_sem.at[0])
    to_scalar.start()

    line = iota((8 * SECTIONS, CPD), 0)
    slot_of_line = 2 * (line // 8) + lax.rem(line, 2)
    kind_of_line = lax.rem(line, 8) // 2
    picks = dest_row == slot_of_line
    pick_codes = (picks & (kind_of_line == 0)).astype(BF16)
    pick_fronts = (picks & (kind_of_line == 1)).astype(BF16)
    coded = (flags_ref[...] * (row_col + 1)).astype(F32).astype(BF16)
    numbered = jnp.where(iota((CPD, 128), 1) < 64, front_col // 32, lax.rem(front_col, 32)).astype(F32).astype(BF16)
    meta = dot(pick_codes, coded, NN) + dot(pick_fronts, numbered, NN)
    meta_out[...] = meta.reshape(SECTIONS, 8, 128).astype(BF16)

    def pad_rows(ref, source):
        ref[...] = jnp.zeros(ref.shape, ref.dtype)
        for r in range(RC):
            ref[r, 0:HARM, 0:BLK] = source[0, :, r * BLK : (r + 1) * BLK].astype(F32)

    pad_rows(cur, lam_ref)
    ext1[1, 1:5] = cur[...].astype(BF16)

    pl.semaphore_wait(barrier, SECTIONS - 1 + SECTORS - 1 + len(corners))

    def halo(ext, sweep):
        moves = [
            (ext.at[1, 1:5], ext.at[0, 1:5], (1, 0)),
            (ext.at[1, 1:5], ext.at[2, 1:5], (-1, 0)),
            (ext.at[1, 4], ext.at[1, 0], (0, 1)),
            (ext.at[1, 1], ext.at[1, 5], (0, -1)),
            (ext.at[1, 4], ext.at[0, 0], (1, 1)),
            (ext.at[1, 1], ext.at[0, 5], (1, -1)),
            (ext.at[1, 4], ext.at[2, 0], (-1, 1)),
            (ext.at[1, 1], ext.at[2, 5], (-1, -1)),
        ]
        return [
            pltpu.make_async_remote_copy(
                src_ref=source, dst_ref=target, send_sem=halo_send.at[sweep, n], recv_sem=halo_recv.at[sweep, n],
                device_id=around(*way), device_id_type=MESH,
            )
            for n, (source, target, way) in enumerate(moves)
        ]

    halo1 = halo(ext1, 0)
    for copy in halo1:
        copy.start()

    def block_copy(i):
        return pltpu.make_async_remote_copy(
            src_ref=send_buf.at[i], dst_ref=recv_buf.at[i], send_sem=block_send.at[i],
            recv_sem=block_recv.at[i], device_id=(ax_peer(i), ci), device_id_type=MESH,
        )

    to_scalar.wait()

    def fill(buf, i):
        slot = 2 * ax_peer(i)
        buf[i, 0:LEN, :] = contacts_ref[idx_s[0, slot]]
        buf[i, LEN : 2 * LEN, :] = contacts_ref[idx_s[0, slot + 1]]
        buf[i, 2 * LEN : MSG, :] = meta_out[ax_peer(i)]

    def start_block(i, carry):
        fill(send_buf, i)
        block_copy(i).start()
        return carry

    lax.fori_loop(1, WINDOW + 1, start_block, 0)
    fill(recv_buf, 0)

    spot = iota((128, 128), 0)
    mixed = (iota((128, 128), 1) == 4 * lax.rem(spot, 24) + spot // 24) & (spot < BLK)
    mixer = mixed.astype(BF16)
    plain = (iota((128, 128), 1) == spot).astype(BF16)
    table = table_ref[...]
    table_hi = table.astype(BF16)
    table_lo = (table - table_hi.astype(F32)).astype(BF16)

    def spread(rows, order):
        turn = dot(order, rows, NT).astype(BF16)
        return dot(turn, table_hi, NN) + dot(turn, table_lo, NN)

    def split(ref, lanes, value):
        first = value.astype(BF16)
        ref[0:128, lanes] = first
        ref[128:256, lanes] = (value - first.astype(F32)).astype(BF16)

    def twice(x):
        return jnp.concatenate([x, x], axis=1)

    pad_rows(state_pad, state_ref)
    for r in range(RC):
        lanes = slice(r * SAMPLES, (r + 1) * SAMPLES)
        split(xw, lanes, spread(ext1[1, 1 + r], mixer))
        split(yw, lanes, spread(state_pad[r].astype(BF16), plain))
    pad_rows(rhs_buf, rhs_ref)
    wide[...] = jnp.zeros(wide.shape, F32)
    for s in range(NNZ):
        wide[s, :, 0:BLK] = blocks_ref[0, :, s * BLK : (s + 1) * BLK].astype(F32)
    acc[...] = jnp.zeros(acc.shape, F32)
    unpack[...] = jnp.zeros(unpack.shape, F32)

    precond = precond_ref[...]
    harmonic = (iota((48, BLK), 0) // 2 + 1).astype(F32) * omega_rate
    mass_term = harmonic * harmonic * mass_ref[...]

    def stiffness(ext):
        total = jnp.zeros((RC * 48, BLK), F32)
        for s in range(NNZ):
            code = slots_ref[0, s]
            rows = ext[code // 3, pl.ds(lax.rem(code, 3), RC)].reshape(RC * 48, 128)
            total = total + dot(rows, wide[s].astype(BF16), NT)
        return total

    def finish_halo(ext, copies):
        for copy in copies:
            copy.wait_recv()

        @pl.when(ax == 0)
        def _():
            ext[0] = jnp.zeros(ext.shape[1:], BF16)

        @pl.when(ax == SECTIONS - 1)
        def _():
            ext[2] = jnp.zeros(ext.shape[1:], BF16)

    def smooth(ext):
        total = stiffness(ext)
        for r in range(RC):
            now = cur[r, :, 0:BLK]
            applied = total[r * 48 : (r + 1) * 48] - mass_term * now
            base[r, :, 0:BLK] = now + precond * (rhs_buf[r, :, 0:BLK] - applied)

    finish_halo(ext1, halo1)
    base[...] = jnp.zeros(base.shape, F32)
    smooth(ext1)

    def masks(k):
        code = codes[pl.ds(k, 1), :]
        return [(code == float(r + 1)).astype(F32) for r in range(RC)]

    def take(i):
        meta = recv_buf[i, 2 * LEN : MSG, :].astype(F32)
        codes[pl.ds(2 * i, 2), :] = meta[0:2]
        fronts[pl.ds(2 * i, 2), :] = meta[2:4]
        for j in range(2):
            k = 2 * i + j
            pieces = [recv_buf[i, LEN * j + 24 * c : LEN * j + 24 * c + 24, :] for c in range(3)]
            square = jnp.concatenate(pieces, axis=1).astype(F32)
            for c in range(4):
                unpack[j, 24 * c : 24 * c + 24, 0:BLK] = square[:, c * BLK : (c + 1) * BLK]
            square = unpack[j]
            flat = square[0:BLK].astype(BF16)
            turn = square.T[0:BLK].astype(BF16)
            turned[k] = turn
            mask = [(meta[j : j + 1] == float(r + 1)).astype(F32) for r in range(RC)]
            forward = dot(twice(flat), yw[...], NN)
            backward = dot(twice(turn), xw[...], NN)
            kept = jnp.zeros((BLK, SAMPLES), F32)
            for r in range(RC):
                lanes = slice(r * SAMPLES, (r + 1) * SAMPLES)
                kept = kept + forward[:, lanes] * mask[r]
                acc[:, lanes] += backward[:, lanes] * mask[r]
            chosen[k] = kept

    take(0)

    def pass_on(i, carry):
        block_copy(i).wait_send()
        start_block(i + WINDOW, carry)
        block_copy(i).wait_recv()
        take(i)
        return carry

    def take_next(i, carry):
        block_copy(i).wait_recv()
        take(i)
        return carry

    lax.fori_loop(1, SECTIONS - WINDOW, pass_on, 0)
    lax.fori_loop(SECTIONS - WINDOW, SECTIONS, take_next, 0)

    def settle(r):
        lanes = slice(r * SAMPLES, (r + 1) * SAMPLES)
        effect = dot(table, acc[:, lanes], NT, HIGHEST) * (2.0 / SAMPLES)
        return base[r, :, 0:BLK] - precond * effect

    for r in range(RC):
        cur[r, :, 0:BLK] = settle(r)
    ext2[1, 1:5] = cur[...].astype(BF16)
    halo2 = halo(ext2, 1)
    for copy in halo2:
        copy.start()
    for r in range(RC):
        lanes = slice(r * SAMPLES, (r + 1) * SAMPLES)
        split(xw, lanes, spread(ext2[1, 1 + r], mixer))

    acc[...] = jnp.zeros(acc.shape, F32)

    def again(g, carry):
        k = g * GROUP
        lhs = turned[pl.ds(k, GROUP)].reshape(GROUP * BLK, 128)
        product = dot(twice(lhs), xw[...], NN)
        mask = [masks(k + j) for j in range(GROUP)]
        for r in range(RC):
            lanes = slice(r * SAMPLES, (r + 1) * SAMPLES)
            total = acc[:, lanes]
            for j in range(GROUP):
                total = total + product[j * BLK : (j + 1) * BLK, lanes] * mask[j][r]
            acc[:, lanes] = total
        return carry

    lax.fori_loop(0, SLOTS // GROUP, again, 0)
    eye128 = (spot == iota((128, 128), 1)).astype(F32)
    high, low = fronts[:, 0:1], fronts[:, 64:65]
    major = jnp.floor(high * 0.25)
    minor = (high - 4.0 * major) * 32.0 + low
    onehot_lo[...] = (minor == iota((128, 128), 1).astype(F32)).astype(F32)
    major_row = jnp.sum(eye128 * major, axis=0, keepdims=True)
    onehot_hi[...] = (major_row == iota((8, 128), 0).astype(F32)).astype(F32)
    finish_halo(ext2, halo2)
    smooth(ext2)
    for r in range(RC):
        final = settle(r)
        adj_ref[0, :, r * BLK : (r + 1) * BLK] = final[0:HARM]
        cur[r, :, 0:BLK] = final
    for r in range(RC):
        bw[r] = spread(cur[r].astype(BF16), mixer)[0:BLK]

    def part(g, carry):
        for j in range(4):
            k = 4 * g + j
            code = jnp.broadcast_to(codes[pl.ds(k, 1), :], (BLK, SAMPLES))
            weight = jnp.where(code == 1.0, bw[0], jnp.where(code == 2.0, bw[1], jnp.where(code == 3.0, bw[2], bw[3])))
            sums[pl.ds(k, 1), :] = jnp.sum(chosen[k] * weight, axis=0, keepdims=True)
        return carry

    lax.fori_loop(0, SLOTS // 4, part, 0)
    parts = jnp.sum(sums[...], axis=1, keepdims=True) * (-sens_scale * 2.0 / SAMPLES)
    own = dot(onehot_hi[...], onehot_lo[...] * parts, NN, HIGHEST)

    def everyone(peers, me, out_of, into, send, recv):
        def copies(j):
            there = lax.rem(me + j, 8)
            going = pltpu.make_async_remote_copy(
                src_ref=out_of(there), dst_ref=into.at[me], send_sem=send.at[j], recv_sem=recv.at[me],
                device_id=peers(there), device_id_type=MESH,
            )
            coming = pltpu.make_async_remote_copy(
                src_ref=out_of(there), dst_ref=into.at[there], send_sem=send.at[j], recv_sem=recv.at[there],
                device_id=peers(there), device_id_type=MESH,
            )
            return going, coming

        pairs = [copies(j) for j in range(1, 8)]
        for going, _ in pairs:
            going.start()
        for _, coming in pairs:
            coming.wait_recv()
        total = into[0]
        for n in range(1, 8):
            total = total + into[n]
        return total, [going for going, _ in pairs]

    part_a[...] = own
    recv_a[ci] = own
    total, sent_a = everyone(lambda j: (ax, j), ci, lambda j: part_a, recv_a, a_send, a_recv)
    for n in range(8):
        part_b[n] = total[n : n + 1]
    recv_b[xy] = part_b[xy]
    total, sent_b = everyone(lambda j: (j * 8 + zz, ci), xy, lambda j: part_b.at[j], recv_b, b_send, b_recv)
    part_c[...] = total
    recv_c[zz] = total
    total, sent_c = everyone(lambda j: (xy * 8 + j, ci), zz, lambda j: part_c, recv_c, c_send, c_recv)
    sens_ref[...] = pltpu.roll(jnp.broadcast_to(total, (8, 128)), lax.rem(128 - 16 * zz, 128), 1)

    for copy in halo1 + halo2 + sent_a + sent_b + sent_c:
        copy.wait_send()

    def drain(i, carry):
        block_copy(i).wait_send()
        return carry

    lax.fori_loop(SECTIONS - WINDOW, SECTIONS, drain, 0)


def shards(
    lam_start, rhs, state, blocks, slots, mass, precond, contact_blocks, contact_flags,
    contact_owner, contact_row, contact_front,
):
    packed = contact_blocks.reshape(CPD, 24, 3, 128).transpose(0, 2, 1, 3).reshape(CPD, LEN, 128)
    table = jnp.asarray(time_table())
    vmem = pl.BlockSpec(memory_space=pltpu.VMEM)
    smem = pl.BlockSpec(memory_space=pltpu.SMEM)
    dma = pltpu.SemaphoreType.DMA
    scratch = [
        pltpu.VMEM((8, SLOTS), jnp.int32),
        pltpu.SMEM((8, SLOTS), jnp.int32),
        pltpu.VMEM((SECTIONS, 8, 128), BF16),
        pltpu.VMEM((SECTIONS, MSG, 128), BF16),
        pltpu.VMEM((SECTIONS, MSG, 128), BF16),
        pltpu.VMEM((2, 128, 128), F32),
        pltpu.VMEM((SLOTS, BLK, 128), BF16),
        pltpu.VMEM((SLOTS, BLK, SAMPLES), F32),
        pltpu.VMEM((BLK, RC * SAMPLES), F32),
        pltpu.VMEM((SLOTS, 128), F32),
        pltpu.VMEM((SLOTS, 128), F32),
        pltpu.VMEM((SLOTS, 128), F32),
        pltpu.VMEM((8, SLOTS), F32),
        pltpu.VMEM((RC, 48, 128), F32),
        pltpu.VMEM((RC, 48, 128), F32),
        pltpu.VMEM((RC, 48, 128), F32),
        pltpu.VMEM((3, 6, 48, 128), BF16),
        pltpu.VMEM((3, 6, 48, 128), BF16),
        pltpu.VMEM((NNZ, BLK, 128), F32),
        pltpu.VMEM((RC, 48, 128), F32),
        pltpu.VMEM((256, RC * SAMPLES), BF16),
        pltpu.VMEM((256, RC * SAMPLES), BF16),
        pltpu.VMEM((RC, BLK, SAMPLES), F32),
        pltpu.VMEM((SLOTS, 128), F32),
        pltpu.VMEM((8, 128), F32),
        pltpu.VMEM((8, 8, 128), F32),
        pltpu.VMEM((8, 1, 128), F32),
        pltpu.VMEM((8, 1, 128), F32),
        pltpu.VMEM((1, 128), F32),
        pltpu.VMEM((8, 1, 128), F32),
        dma((1,)), dma((SECTIONS,)), dma((SECTIONS,)),
        dma((2, 8)), dma((2, 8)), dma((8,)), dma((8,)), dma((8,)), dma((8,)), dma((8,)), dma((8,)),
    ]
    adjoint, sums = pl.pallas_call(
        kernel,
        out_shape=(
            jax.ShapeDtypeStruct((1, HARM, RC * BLK), F32),
            jax.ShapeDtypeStruct((8, 128), F32),
        ),
        in_specs=[vmem, vmem, vmem, vmem, smem] + [vmem] * 8,
        out_specs=(vmem, vmem),
        scratch_shapes=scratch,
        compiler_params=pltpu.CompilerParams(
            collective_id=0, has_side_effects=True, vmem_limit_bytes=56 * 2**20
        ),
        cost_estimate=pl.CostEstimate(flops=4 * 10**9, bytes_accessed=3 * 10**6, transcendentals=0),
    )(
        lam_start, rhs, state, blocks, slots, mass, precond, packed, contact_flags,
        contact_owner.reshape(1, CPD), contact_row.reshape(1, CPD), contact_front.reshape(1, CPD), table,
    )
    return adjoint, sums[0, :16]


def solution(mesh):
    in_specs = (
        P("ax", None, "circ"),
        P("ax", None, "circ"),
        P("ax", None, "circ"),
        P("ax", None, None),
        P("ax", None),
        P("ax", None),
        P("ax", None),
        P(("ax", "circ"), None),
        P(("ax", "circ"), None),
        P(("ax", "circ")),
        P(("ax", "circ")),
        P(("ax", "circ")),
    )
    out_specs = (P("ax", None, "circ"), P("ax"))
    return jax.shard_map(shards, mesh=mesh, in_specs=in_specs, out_specs=out_specs, check_vma=False)
```

```python
import math

import jax
import jax.numpy as jnp
import numpy as np
from jax import lax
from jax.experimental import pallas as pl
from jax.experimental.pallas import tpu as pltpu
from jax.sharding import PartitionSpec as P

BLK = 96
HARM = 42
SAMPLES = 128
NNZ = 8
RC = 4
CPD = 64
SECTIONS = 64
SECTORS = 8
SLOTS = 2 * SECTIONS
STEP = 29
GROUP = 8
WINDOW = 16
EARLY = 20
LEN = 72
MSG = 2 * LEN + 8

omega_rate = 0.05
sens_scale = 0.015625

F32 = jnp.float32
BF16 = jnp.bfloat16
HIGHEST = lax.Precision.HIGHEST
MESH = pl.DeviceIdType.MESH


def time_table():
    moments = np.arange(SAMPLES)[:, None]
    columns = np.arange(48)[None, :]
    phases = (2.0 * math.pi / SAMPLES) * ((moments * (columns // 2 + 1)) % SAMPLES)
    rows = np.where(columns % 2 == 0, np.cos(phases), np.sin(phases))
    rows[:, HARM:] = 0.0
    return rows.T.astype(np.float32)


def iota(shape, dim):
    return lax.broadcasted_iota(jnp.int32, shape, dim)


def dot(a, b, dims, precision=None):
    return lax.dot_general(a, b, (dims, ((), ())), precision=precision, preferred_element_type=F32)


NT = ((1,), (1,))
NN = ((1,), (0,))


def kernel(
    lam_ref, rhs_ref, state_ref, blocks_ref, slots_ref, mass_ref, precond_ref, contacts_ref,
    flags_ref, owner_ref, row_ref, front_ref, table_ref,
    adj_ref, sens_ref,
    idx_v, idx_s, meta_out, send_buf, recv_buf, unpack, turned, chosen, acc, codes, fronts,
    onehot_lo, onehot_hi, rhs_buf, cur, base, ext1, ext2, wide, state_pad, xw, yw, tables, bw, sums,
    part_a, recv_a, part_b, recv_b, part_c, recv_c,
    local_sem, block_send, block_recv, halo_send, halo_recv,
    a_send, a_recv, b_send, b_recv, c_send, c_recv,
):
    ax = lax.axis_index("ax")
    ci = lax.axis_index("circ")
    xy, zz = ax // 8, lax.rem(ax, 8)

    def offset(i):
        return lax.rem(i * STEP, SECTIONS)

    def ax_peer(i):
        return lax.rem(ax + offset(i), SECTIONS)

    def around(da, dc):
        return (lax.rem(ax + da + SECTIONS, SECTIONS), lax.rem(ci + dc + SECTORS, SECTORS))

    corners = [(1, 1), (1, -1), (-1, 1), (-1, -1)]
    barrier = pltpu.get_barrier_semaphore()

    def greet(i, carry):
        pl.semaphore_signal(barrier, inc=1, device_id=(ax_peer(i), ci), device_id_type=MESH)
        return carry

    lax.fori_loop(1, SECTIONS, greet, 0)

    def greet_circ(j, carry):
        pl.semaphore_signal(barrier, inc=1, device_id=(ax, lax.rem(ci + j, SECTORS)), device_id_type=MESH)
        return carry

    lax.fori_loop(1, SECTORS, greet_circ, 0)
    for da, dc in corners:
        pl.semaphore_signal(barrier, inc=1, device_id=around(da, dc), device_id_type=MESH)

    eye64 = (iota((CPD, CPD), 0) == iota((CPD, CPD), 1)).astype(jnp.int32)

    def column(row):
        return jnp.sum(eye64 * row, axis=1, keepdims=True)

    owner_row = owner_ref[...]
    owner_col = column(owner_row)
    row_col = column(row_ref[...])
    front_col = column(front_ref[...])
    same = (owner_col == owner_row).astype(jnp.int32)
    below = (iota((CPD, CPD), 0) < iota((CPD, CPD), 1)).astype(jnp.int32)
    above = (iota((CPD, CPD), 1) < iota((CPD, CPD), 0)).astype(jnp.int32)
    dest_row = 2 * owner_row + jnp.sum(same * below, axis=0, keepdims=True)
    dest_col = 2 * owner_col + jnp.sum(same * above, axis=1, keepdims=True)
    hit = (dest_col == iota((CPD, SLOTS), 1)).astype(jnp.int32)
    index_row = jnp.sum(hit * iota((CPD, SLOTS), 0), axis=0, keepdims=True)
    idx_v[...] = jnp.broadcast_to(index_row, (8, SLOTS))
    to_scalar = pltpu.make_async_copy(idx_v, idx_s, local_sem.at[0])
    to_scalar.start()

    line = iota((8 * SECTIONS, CPD), 0)
    slot_of_line = 2 * (line // 8) + lax.rem(line, 2)
    kind_of_line = lax.rem(line, 8) // 2
    picks = dest_row == slot_of_line
    pick_codes = (picks & (kind_of_line == 0)).astype(BF16)
    pick_fronts = (picks & (kind_of_line == 1)).astype(BF16)
    coded = (flags_ref[...] * (row_col + 1)).astype(F32).astype(BF16)
    numbered = jnp.where(iota((CPD, 128), 1) < 64, front_col // 32, lax.rem(front_col, 32)).astype(F32).astype(BF16)
    meta = dot(pick_codes, coded, NN) + dot(pick_fronts, numbered, NN)
    meta_out[...] = meta.reshape(SECTIONS, 8, 128).astype(BF16)

    def pad_rows(ref, source):
        ref[...] = jnp.zeros(ref.shape, ref.dtype)
        for r in range(RC):
            ref[r, 0:HARM, 0:BLK] = source[0, :, r * BLK : (r + 1) * BLK].astype(F32)

    pad_rows(cur, lam_ref)
    ext1[1, 1:5] = cur[...].astype(BF16)

    pl.semaphore_wait(barrier, SECTIONS - 1 + SECTORS - 1 + len(corners))

    def halo(ext, sweep):
        moves = [
            (ext.at[1, 1:5], ext.at[0, 1:5], (1, 0)),
            (ext.at[1, 1:5], ext.at[2, 1:5], (-1, 0)),
            (ext.at[1, 4], ext.at[1, 0], (0, 1)),
            (ext.at[1, 1], ext.at[1, 5], (0, -1)),
            (ext.at[1, 4], ext.at[0, 0], (1, 1)),
            (ext.at[1, 1], ext.at[0, 5], (1, -1)),
            (ext.at[1, 4], ext.at[2, 0], (-1, 1)),
            (ext.at[1, 1], ext.at[2, 5], (-1, -1)),
        ]
        return [
            pltpu.make_async_remote_copy(
                src_ref=source, dst_ref=target, send_sem=halo_send.at[sweep, n], recv_sem=halo_recv.at[sweep, n],
                device_id=around(*way), device_id_type=MESH,
            )
            for n, (source, target, way) in enumerate(moves)
        ]

    halo1 = halo(ext1, 0)
    for copy in halo1:
        copy.start()

    def block_copy(i):
        return pltpu.make_async_remote_copy(
            src_ref=send_buf.at[i], dst_ref=recv_buf.at[i], send_sem=block_send.at[i],
            recv_sem=block_recv.at[i], device_id=(ax_peer(i), ci), device_id_type=MESH,
        )

    to_scalar.wait()

    def fill(buf, i):
        slot = 2 * ax_peer(i)
        buf[i, 0:LEN, :] = contacts_ref[idx_s[0, slot]]
        buf[i, LEN : 2 * LEN, :] = contacts_ref[idx_s[0, slot + 1]]
        buf[i, 2 * LEN : MSG, :] = meta_out[ax_peer(i)]

    def start_block(i, carry):
        fill(send_buf, i)
        block_copy(i).start()
        return carry

    lax.fori_loop(1, WINDOW + 1, start_block, 0)
    fill(recv_buf, 0)

    spot = iota((128, 128), 0)
    mixed = (iota((128, 128), 1) == 4 * lax.rem(spot, 24) + spot // 24) & (spot < BLK)
    mixer = mixed.astype(BF16)
    plain = (iota((128, 128), 1) == spot).astype(BF16)
    table = table_ref[...]
    table_hi = table.astype(BF16)
    table_lo = (table - table_hi.astype(F32)).astype(BF16)

    tables[...] = jnp.zeros(tables.shape, BF16)
    for r in range(RC):
        tables[0, 48 * r : 48 * r + 48, r * SAMPLES : (r + 1) * SAMPLES] = table_hi
        tables[1, 48 * r : 48 * r + 48, r * SAMPLES : (r + 1) * SAMPLES] = table_lo

    def spread(rows, order):
        turn = dot(order, rows.reshape(RC * 48, 128), NT).astype(BF16)
        return dot(turn, tables[0], NN) + dot(turn, tables[1], NN)

    def split(ref, value):
        first = value.astype(BF16)
        ref[0:128, :] = first
        ref[128:256, :] = (value - first.astype(F32)).astype(BF16)

    def twice(x):
        return jnp.concatenate([x, x], axis=1)

    pad_rows(state_pad, state_ref)
    split(xw, spread(ext1[1, 1:5], mixer))
    split(yw, spread(state_pad[...].astype(BF16), plain))
    acc[...] = jnp.zeros(acc.shape, F32)
    unpack[...] = jnp.zeros(unpack.shape, F32)

    precond = precond_ref[...]
    harmonic = (iota((48, BLK), 0) // 2 + 1).astype(F32) * omega_rate
    mass_term = harmonic * harmonic * mass_ref[...]

    def stiffness(ext):
        total = jnp.zeros((RC * 48, BLK), F32)
        for s in range(NNZ):
            code = slots_ref[0, s]
            rows = ext[code // 3, pl.ds(lax.rem(code, 3), RC)].reshape(RC * 48, 128)
            total = total + dot(rows, wide[s].astype(BF16), NT)
        return total

    def finish_halo(ext, copies):
        for copy in copies:
            copy.wait_recv()

        @pl.when(ax == 0)
        def _():
            ext[0] = jnp.zeros(ext.shape[1:], BF16)

        @pl.when(ax == SECTIONS - 1)
        def _():
            ext[2] = jnp.zeros(ext.shape[1:], BF16)

    def smooth(ext):
        total = stiffness(ext)
        for r in range(RC):
            now = cur[r, :, 0:BLK]
            applied = total[r * 48 : (r + 1) * 48] - mass_term * now
            base[r, :, 0:BLK] = now + precond * (rhs_buf[r, :, 0:BLK] - applied)

    def masks(k):
        code = codes[pl.ds(k, 1), :]
        return [(code == float(r + 1)).astype(F32) for r in range(RC)]

    def take(i):
        meta = recv_buf[i, 2 * LEN : MSG, :].astype(F32)
        codes[pl.ds(2 * i, 2), :] = meta[0:2]
        fronts[pl.ds(2 * i, 2), :] = meta[2:4]
        for j in range(2):
            k = 2 * i + j
            pieces = [recv_buf[i, LEN * j + 24 * c : LEN * j + 24 * c + 24, :] for c in range(3)]
            square = jnp.concatenate(pieces, axis=1).astype(F32)
            for c in range(4):
                unpack[j, 24 * c : 24 * c + 24, 0:BLK] = square[:, c * BLK : (c + 1) * BLK]
            square = unpack[j]
            flat = square[0:BLK].astype(BF16)
            turn = square.T[0:BLK].astype(BF16)
            turned[k] = turn
            mask = [(meta[j : j + 1] == float(r + 1)).astype(F32) for r in range(RC)]
            forward = dot(twice(flat), yw[...], NN)
            backward = dot(twice(turn), xw[...], NN)
            kept = jnp.zeros((BLK, SAMPLES), F32)
            for r in range(RC):
                lanes = slice(r * SAMPLES, (r + 1) * SAMPLES)
                kept = kept + forward[:, lanes] * mask[r]
                acc[:, lanes] += backward[:, lanes] * mask[r]
            chosen[k] = kept

    take(0)

    def pass_on(i, carry):
        block_copy(i).wait_send()
        start_block(i + WINDOW, carry)
        block_copy(i).wait_recv()
        take(i)
        return carry

    def take_next(i, carry):
        block_copy(i).wait_recv()
        take(i)
        return carry

    lax.fori_loop(1, EARLY, pass_on, 0)
    pad_rows(rhs_buf, rhs_ref)
    wide[...] = jnp.zeros(wide.shape, F32)
    for s in range(NNZ):
        wide[s, :, 0:BLK] = blocks_ref[0, :, s * BLK : (s + 1) * BLK].astype(F32)
    finish_halo(ext1, halo1)
    smooth(ext1)
    lax.fori_loop(EARLY, SECTIONS - WINDOW, pass_on, 0)
    lax.fori_loop(SECTIONS - WINDOW, SECTIONS, take_next, 0)

    def settle():
        rows = jnp.concatenate([acc[:, r * SAMPLES : (r + 1) * SAMPLES] for r in range(RC)], axis=0)
        first = rows.astype(BF16)
        second = (rows - first.astype(F32)).astype(BF16)
        left = jnp.concatenate([table_hi, table_lo, table_hi], axis=1)
        effect = dot(left, jnp.concatenate([first, first, second], axis=1), NT) * (2.0 / SAMPLES)
        return [base[r, :, 0:BLK] - precond * effect[:, r * BLK : (r + 1) * BLK] for r in range(RC)]

    for r, value in enumerate(settle()):
        cur[r, :, 0:BLK] = value
    ext2[1, 1:5] = cur[...].astype(BF16)
    halo2 = halo(ext2, 1)
    for copy in halo2:
        copy.start()
    split(xw, spread(ext2[1, 1:5], mixer))
    acc[...] = jnp.zeros(acc.shape, F32)

    def again(g, carry):
        k = g * GROUP
        lhs = turned[pl.ds(k, GROUP)].reshape(GROUP * BLK, 128)
        product = dot(twice(lhs), xw[...], NN)
        mask = [masks(k + j) for j in range(GROUP)]
        for r in range(RC):
            lanes = slice(r * SAMPLES, (r + 1) * SAMPLES)
            total = acc[:, lanes]
            for j in range(GROUP):
                total = total + product[j * BLK : (j + 1) * BLK, lanes] * mask[j][r]
            acc[:, lanes] = total
        return carry

    lax.fori_loop(0, SLOTS // GROUP, again, 0)
    eye128 = (spot == iota((128, 128), 1)).astype(F32)
    high, low = fronts[:, 0:1], fronts[:, 64:65]
    major = jnp.floor(high * 0.25)
    minor = (high - 4.0 * major) * 32.0 + low
    onehot_lo[...] = (minor == iota((128, 128), 1).astype(F32)).astype(F32)
    major_row = jnp.sum(eye128 * major, axis=0, keepdims=True)
    onehot_hi[...] = (major_row == iota((8, 128), 0).astype(F32)).astype(F32)
    finish_halo(ext2, halo2)
    smooth(ext2)
    for r, value in enumerate(settle()):
        adj_ref[0, :, r * BLK : (r + 1) * BLK] = value[0:HARM]
        cur[r, :, 0:BLK] = value
    bw[...] = spread(cur[...].astype(BF16), mixer)[0:BLK]

    def part(g, carry):
        for j in range(4):
            k = 4 * g + j
            code = jnp.broadcast_to(codes[pl.ds(k, 1), :], (BLK, SAMPLES))
            rows = [bw[:, r * SAMPLES : (r + 1) * SAMPLES] for r in range(RC)]
            weight = jnp.where(code == 1.0, rows[0], jnp.where(code == 2.0, rows[1], jnp.where(code == 3.0, rows[2], rows[3])))
            sums[pl.ds(k, 1), :] = jnp.sum(chosen[k] * weight, axis=0, keepdims=True)
        return carry

    lax.fori_loop(0, SLOTS // 4, part, 0)
    parts = jnp.sum(sums[...], axis=1, keepdims=True) * (-sens_scale * 2.0 / SAMPLES)
    own = dot(onehot_hi[...], onehot_lo[...] * parts, NN, HIGHEST)

    def everyone(peers, me, out_of, into, send, recv):
        def copies(j):
            there = lax.rem(me + j, 8)
            going = pltpu.make_async_remote_copy(
                src_ref=out_of(there), dst_ref=into.at[me], send_sem=send.at[j], recv_sem=recv.at[me],
                device_id=peers(there), device_id_type=MESH,
            )
            coming = pltpu.make_async_remote_copy(
                src_ref=out_of(there), dst_ref=into.at[there], send_sem=send.at[j], recv_sem=recv.at[there],
                device_id=peers(there), device_id_type=MESH,
            )
            return going, coming

        pairs = [copies(j) for j in range(1, 8)]
        for going, _ in pairs:
            going.start()
        for _, coming in pairs:
            coming.wait_recv()
        total = into[0]
        for n in range(1, 8):
            total = total + into[n]
        return total, [going for going, _ in pairs]

    part_a[...] = own
    recv_a[ci] = own
    total, sent_a = everyone(lambda j: (ax, j), ci, lambda j: part_a, recv_a, a_send, a_recv)
    for n in range(8):
        part_b[n] = total[n : n + 1]
    recv_b[xy] = part_b[xy]
    total, sent_b = everyone(lambda j: (j * 8 + zz, ci), xy, lambda j: part_b.at[j], recv_b, b_send, b_recv)
    part_c[...] = total
    recv_c[zz] = total
    total, sent_c = everyone(lambda j: (xy * 8 + j, ci), zz, lambda j: part_c, recv_c, c_send, c_recv)
    sens_ref[...] = pltpu.roll(jnp.broadcast_to(total, (8, 128)), lax.rem(128 - 16 * zz, 128), 1)

    for copy in halo1 + halo2 + sent_a + sent_b + sent_c:
        copy.wait_send()

    def drain(i, carry):
        block_copy(i).wait_send()
        return carry

    lax.fori_loop(SECTIONS - WINDOW, SECTIONS, drain, 0)


def finish(adj_ref, sums_ref, adj_out, sens_out):
    adj_out[:, 0, :] = adj_ref[0]
    sens_out[...] = sums_ref[0, 0:16]


def shards(
    lam_start, rhs, state, blocks, slots, mass, precond, contact_blocks, contact_flags,
    contact_owner, contact_row, contact_front,
):
    packed = contact_blocks.reshape(CPD, 24, 3, 128).transpose(0, 2, 1, 3).reshape(CPD, LEN, 128)
    table = jnp.asarray(time_table())
    vmem = pl.BlockSpec(memory_space=pltpu.VMEM)
    smem = pl.BlockSpec(memory_space=pltpu.SMEM)
    dma = pltpu.SemaphoreType.DMA
    scratch = [
        pltpu.VMEM((8, SLOTS), jnp.int32),
        pltpu.SMEM((8, SLOTS), jnp.int32),
        pltpu.VMEM((SECTIONS, 8, 128), BF16),
        pltpu.VMEM((SECTIONS, MSG, 128), BF16),
        pltpu.VMEM((SECTIONS, MSG, 128), BF16),
        pltpu.VMEM((2, 128, 128), F32),
        pltpu.VMEM((SLOTS, BLK, 128), BF16),
        pltpu.VMEM((SLOTS, BLK, SAMPLES), F32),
        pltpu.VMEM((BLK, RC * SAMPLES), F32),
        pltpu.VMEM((SLOTS, 128), F32),
        pltpu.VMEM((SLOTS, 128), F32),
        pltpu.VMEM((SLOTS, 128), F32),
        pltpu.VMEM((8, SLOTS), F32),
        pltpu.VMEM((RC, 48, 128), F32),
        pltpu.VMEM((RC, 48, 128), F32),
        pltpu.VMEM((RC, 48, 128), F32),
        pltpu.VMEM((3, 6, 48, 128), BF16),
        pltpu.VMEM((3, 6, 48, 128), BF16),
        pltpu.VMEM((NNZ, BLK, 128), F32),
        pltpu.VMEM((RC, 48, 128), F32),
        pltpu.VMEM((256, RC * SAMPLES), BF16),
        pltpu.VMEM((256, RC * SAMPLES), BF16),
        pltpu.VMEM((2, RC * 48, RC * SAMPLES), BF16),
        pltpu.VMEM((BLK, RC * SAMPLES), F32),
        pltpu.VMEM((SLOTS, 128), F32),
        pltpu.VMEM((8, 128), F32),
        pltpu.VMEM((8, 8, 128), F32),
        pltpu.VMEM((8, 1, 128), F32),
        pltpu.VMEM((8, 1, 128), F32),
        pltpu.VMEM((1, 128), F32),
        pltpu.VMEM((8, 1, 128), F32),
        dma((1,)), dma((SECTIONS,)), dma((SECTIONS,)),
        dma((2, 8)), dma((2, 8)), dma((8,)), dma((8,)), dma((8,)), dma((8,)), dma((8,)), dma((8,)),
    ]
    adjoint, sums = pl.pallas_call(
        kernel,
        out_shape=(
            jax.ShapeDtypeStruct((1, HARM, RC * BLK), F32),
            jax.ShapeDtypeStruct((8, 128), F32),
        ),
        in_specs=[vmem, vmem, vmem, vmem, smem] + [vmem] * 8,
        out_specs=(vmem, vmem),
        scratch_shapes=scratch,
        compiler_params=pltpu.CompilerParams(
            collective_id=0, has_side_effects=True, vmem_limit_bytes=56 * 2**20
        ),
        cost_estimate=pl.CostEstimate(flops=4 * 10**9, bytes_accessed=3 * 10**6, transcendentals=0),
    )(
        lam_start, rhs, state, blocks, slots, mass, precond, packed, contact_flags,
        contact_owner.reshape(1, CPD), contact_row.reshape(1, CPD), contact_front.reshape(1, CPD), table,
    )
    adjoint, sums = pl.pallas_call(
        finish,
        out_shape=(
            jax.ShapeDtypeStruct((HARM, 1, RC * BLK), F32),
            jax.ShapeDtypeStruct((16,), F32),
        ),
        in_specs=[vmem, vmem],
        out_specs=(vmem, vmem),
    )(adjoint, sums)
    return adjoint.transpose(1, 0, 2), sums


def solution(mesh):
    in_specs = (
        P("ax", None, "circ"),
        P("ax", None, "circ"),
        P("ax", None, "circ"),
        P("ax", None, None),
        P("ax", None),
        P("ax", None),
        P("ax", None),
        P(("ax", "circ"), None),
        P(("ax", "circ"), None),
        P(("ax", "circ")),
        P(("ax", "circ")),
        P(("ax", "circ")),
    )
    out_specs = (P("ax", None, "circ"), P("ax"))
    return jax.shard_map(shards, mesh=mesh, in_specs=in_specs, out_specs=out_specs, check_vma=False)
```

```python
import math

import jax
import jax.numpy as jnp
import numpy as np
from jax import lax
from jax.experimental import pallas as pl
from jax.experimental.pallas import tpu as pltpu
from jax.sharding import PartitionSpec as P

BLK = 96
HARM = 42
SAMPLES = 128
NNZ = 8
RC = 4
CPD = 64
SECTIONS = 64
SECTORS = 8
SLOTS = 2 * SECTIONS
STEP = 29
GROUP = 8
WINDOW = 16
EARLY = 20
LEN = 72
MSG = 2 * LEN + 8

omega_rate = 0.05
sens_scale = 0.015625

F32 = jnp.float32
BF16 = jnp.bfloat16
HIGHEST = lax.Precision.HIGHEST
MESH = pl.DeviceIdType.MESH


def time_table():
    moments = np.arange(SAMPLES)[:, None]
    columns = np.arange(48)[None, :]
    phases = (2.0 * math.pi / SAMPLES) * ((moments * (columns // 2 + 1)) % SAMPLES)
    rows = np.where(columns % 2 == 0, np.cos(phases), np.sin(phases))
    rows[:, HARM:] = 0.0
    return rows.T.astype(np.float32)


def iota(shape, dim):
    return lax.broadcasted_iota(jnp.int32, shape, dim)


def dot(a, b, dims, precision=None):
    return lax.dot_general(a, b, (dims, ((), ())), precision=precision, preferred_element_type=F32)


NT = ((1,), (1,))
NN = ((1,), (0,))


def kernel(
    lam_ref, rhs_ref, state_ref, blocks_ref, slots_ref, mass_ref, precond_ref, contacts_ref,
    flags_ref, owner_ref, row_ref, front_ref, table_ref,
    adj_ref, sens_ref,
    idx_v, idx_s, meta_out, send_buf, recv_buf, unpack, turned, chosen, acc, codes, fronts,
    onehot_lo, onehot_hi, rhs_buf, cur, base, ext1, ext2, wide, state_pad, xw, yw, tables, bw, sums,
    part_a, recv_a, part_b, recv_b, part_c, recv_c,
    local_sem, block_send, block_recv, halo_send, halo_recv,
    a_send, a_recv, b_send, b_recv, c_send, c_recv,
):
    ax = lax.axis_index("ax")
    ci = lax.axis_index("circ")
    xy, zz = ax // 8, lax.rem(ax, 8)

    def offset(i):
        return lax.rem(i * STEP, SECTIONS)

    def ax_peer(i):
        return lax.rem(ax + offset(i), SECTIONS)

    def around(da, dc):
        return (lax.rem(ax + da + SECTIONS, SECTIONS), lax.rem(ci + dc + SECTORS, SECTORS))

    corners = [(1, 1), (1, -1), (-1, 1), (-1, -1)]
    barrier = pltpu.get_barrier_semaphore()

    def greet(i, carry):
        pl.semaphore_signal(barrier, inc=1, device_id=(ax_peer(i), ci), device_id_type=MESH)
        return carry

    lax.fori_loop(1, SECTIONS, greet, 0)

    def greet_circ(j, carry):
        pl.semaphore_signal(barrier, inc=1, device_id=(ax, lax.rem(ci + j, SECTORS)), device_id_type=MESH)
        return carry

    lax.fori_loop(1, SECTORS, greet_circ, 0)
    for da, dc in corners:
        pl.semaphore_signal(barrier, inc=1, device_id=around(da, dc), device_id_type=MESH)

    eye64 = (iota((CPD, CPD), 0) == iota((CPD, CPD), 1)).astype(jnp.int32)

    def column(row):
        return jnp.sum(eye64 * row, axis=1, keepdims=True)

    owner_row = owner_ref[...]
    owner_col = column(owner_row)
    row_col = column(row_ref[...])
    front_col = column(front_ref[...])
    same = (owner_col == owner_row).astype(jnp.int32)
    below = (iota((CPD, CPD), 0) < iota((CPD, CPD), 1)).astype(jnp.int32)
    above = (iota((CPD, CPD), 1) < iota((CPD, CPD), 0)).astype(jnp.int32)
    dest_row = 2 * owner_row + jnp.sum(same * below, axis=0, keepdims=True)
    dest_col = 2 * owner_col + jnp.sum(same * above, axis=1, keepdims=True)
    hit = (dest_col == iota((CPD, SLOTS), 1)).astype(jnp.int32)
    index_row = jnp.sum(hit * iota((CPD, SLOTS), 0), axis=0, keepdims=True)
    idx_v[...] = jnp.broadcast_to(index_row, (8, SLOTS))
    to_scalar = pltpu.make_async_copy(idx_v, idx_s, local_sem.at[0])
    to_scalar.start()

    line = iota((8 * SECTIONS, CPD), 0)
    slot_of_line = 2 * (line // 8) + lax.rem(line, 2)
    kind_of_line = lax.rem(line, 8) // 2
    picks = dest_row == slot_of_line
    pick_codes = (picks & (kind_of_line == 0)).astype(BF16)
    pick_fronts = (picks & (kind_of_line == 1)).astype(BF16)
    coded = (flags_ref[...] * (row_col + 1)).astype(F32).astype(BF16)
    numbered = jnp.where(iota((CPD, 128), 1) < 64, front_col // 32, lax.rem(front_col, 32)).astype(F32).astype(BF16)
    meta = dot(pick_codes, coded, NN) + dot(pick_fronts, numbered, NN)
    meta_out[...] = meta.reshape(SECTIONS, 8, 128).astype(BF16)

    def pad_rows(ref, source):
        ref[...] = jnp.zeros(ref.shape, ref.dtype)
        for r in range(RC):
            ref[r, 0:HARM, 0:BLK] = source[0, :, r * BLK : (r + 1) * BLK].astype(F32)

    pad_rows(cur, lam_ref)
    ext1[1, 1:5] = cur[...].astype(BF16)

    pl.semaphore_wait(barrier, SECTIONS - 1 + SECTORS - 1 + len(corners))

    def halo(ext, sweep):
        moves = [
            (ext.at[1, 1:5], ext.at[0, 1:5], (1, 0)),
            (ext.at[1, 1:5], ext.at[2, 1:5], (-1, 0)),
            (ext.at[1, 4], ext.at[1, 0], (0, 1)),
            (ext.at[1, 1], ext.at[1, 5], (0, -1)),
            (ext.at[1, 4], ext.at[0, 0], (1, 1)),
            (ext.at[1, 1], ext.at[0, 5], (1, -1)),
            (ext.at[1, 4], ext.at[2, 0], (-1, 1)),
            (ext.at[1, 1], ext.at[2, 5], (-1, -1)),
        ]
        return [
            pltpu.make_async_remote_copy(
                src_ref=source, dst_ref=target, send_sem=halo_send.at[sweep, n], recv_sem=halo_recv.at[sweep, n],
                device_id=around(*way), device_id_type=MESH,
            )
            for n, (source, target, way) in enumerate(moves)
        ]

    halo1 = halo(ext1, 0)
    for copy in halo1:
        copy.start()

    def block_copy(i):
        return pltpu.make_async_remote_copy(
            src_ref=send_buf.at[i], dst_ref=recv_buf.at[i], send_sem=block_send.at[i],
            recv_sem=block_recv.at[i], device_id=(ax_peer(i), ci), device_id_type=MESH,
        )

    to_scalar.wait()

    def fill(buf, i):
        slot = 2 * ax_peer(i)
        buf[i, 0:LEN, :] = contacts_ref[idx_s[0, slot]]
        buf[i, LEN : 2 * LEN, :] = contacts_ref[idx_s[0, slot + 1]]
        buf[i, 2 * LEN : MSG, :] = meta_out[ax_peer(i)]

    def start_block(i, carry):
        fill(send_buf, i)
        block_copy(i).start()
        return carry

    lax.fori_loop(1, WINDOW + 1, start_block, 0)
    fill(recv_buf, 0)

    spot = iota((128, 128), 0)
    mixed = (iota((128, 128), 1) == 4 * lax.rem(spot, 24) + spot // 24) & (spot < BLK)
    mixer = mixed.astype(BF16)
    plain = (iota((128, 128), 1) == spot).astype(BF16)
    table = table_ref[...]
    table_hi = table.astype(BF16)
    table_lo = (table - table_hi.astype(F32)).astype(BF16)

    tables[...] = jnp.zeros(tables.shape, BF16)
    for r in range(RC):
        tables[0, 48 * r : 48 * r + 48, r * SAMPLES : (r + 1) * SAMPLES] = table_hi
        tables[1, 48 * r : 48 * r + 48, r * SAMPLES : (r + 1) * SAMPLES] = table_lo

    def spread(rows, order):
        turn = dot(order, rows.reshape(RC * 48, 128), NT).astype(BF16)
        return dot(turn, tables[0], NN) + dot(turn, tables[1], NN)

    def split(ref, value):
        first = value.astype(BF16)
        ref[0:128, :] = first
        ref[128:256, :] = (value - first.astype(F32)).astype(BF16)

    def twice(x):
        return jnp.concatenate([x, x], axis=1)

    pad_rows(state_pad, state_ref)
    split(xw, spread(ext1[1, 1:5], mixer))
    split(yw, spread(state_pad[...].astype(BF16), plain))
    acc[...] = jnp.zeros(acc.shape, F32)
    unpack[...] = jnp.zeros(unpack.shape, F32)

    precond = precond_ref[...]
    harmonic = (iota((48, BLK), 0) // 2 + 1).astype(F32) * omega_rate
    mass_term = harmonic * harmonic * mass_ref[...]

    def stiffness(ext):
        total = jnp.zeros((RC * 48, BLK), F32)
        for s in range(NNZ):
            code = slots_ref[0, s]
            rows = ext[code // 3, pl.ds(lax.rem(code, 3), RC)].reshape(RC * 48, 128)
            total = total + dot(rows, wide[s].astype(BF16), NT)
        return total

    def finish_halo(ext, copies):
        for copy in copies:
            copy.wait_recv()

        @pl.when(ax == 0)
        def _():
            ext[0] = jnp.zeros(ext.shape[1:], BF16)

        @pl.when(ax == SECTIONS - 1)
        def _():
            ext[2] = jnp.zeros(ext.shape[1:], BF16)

    def smooth(ext):
        total = stiffness(ext)
        for r in range(RC):
            now = cur[r, :, 0:BLK]
            applied = total[r * 48 : (r + 1) * 48] - mass_term * now
            base[r, :, 0:BLK] = now + precond * (rhs_buf[r, :, 0:BLK] - applied)

    def masks(k):
        code = codes[pl.ds(k, 1), :]
        return [(code == float(r + 1)).astype(F32) for r in range(RC)]

    def take(i):
        meta = recv_buf[i, 2 * LEN : MSG, :].astype(F32)
        codes[pl.ds(2 * i, 2), :] = meta[0:2]
        fronts[pl.ds(2 * i, 2), :] = meta[2:4]
        for j in range(2):
            k = 2 * i + j
            pieces = [recv_buf[i, LEN * j + 24 * c : LEN * j + 24 * c + 24, :] for c in range(3)]
            square = jnp.concatenate(pieces, axis=1).astype(F32)
            for c in range(4):
                unpack[j, 24 * c : 24 * c + 24, 0:BLK] = square[:, c * BLK : (c + 1) * BLK]
            square = unpack[j]
            flat = square[0:BLK].astype(BF16)
            turn = square.T[0:BLK].astype(BF16)
            turned[k] = turn
            mask = [(meta[j : j + 1] == float(r + 1)).astype(F32) for r in range(RC)]
            forward = dot(twice(flat), yw[...], NN)
            backward = dot(twice(turn), xw[...], NN)
            kept = jnp.zeros((BLK, SAMPLES), F32)
            for r in range(RC):
                lanes = slice(r * SAMPLES, (r + 1) * SAMPLES)
                kept = kept + forward[:, lanes] * mask[r]
                acc[:, lanes] += backward[:, lanes] * mask[r]
            chosen[k] = kept

    take(0)

    def pass_on(i, carry):
        block_copy(i).wait_send()
        start_block(i + WINDOW, carry)
        block_copy(i).wait_recv()
        take(i)
        return carry

    def take_next(i, carry):
        block_copy(i).wait_recv()
        take(i)
        return carry

    lax.fori_loop(1, EARLY, pass_on, 0)
    pad_rows(rhs_buf, rhs_ref)
    wide[...] = jnp.zeros(wide.shape, F32)
    for s in range(NNZ):
        wide[s, :, 0:BLK] = blocks_ref[0, :, s * BLK : (s + 1) * BLK].astype(F32)
    finish_halo(ext1, halo1)
    smooth(ext1)
    lax.fori_loop(EARLY, SECTIONS - WINDOW, pass_on, 0)
    lax.fori_loop(SECTIONS - WINDOW, SECTIONS, take_next, 0)

    def settle():
        rows = jnp.concatenate([acc[:, r * SAMPLES : (r + 1) * SAMPLES] for r in range(RC)], axis=0)
        first = rows.astype(BF16)
        second = (rows - first.astype(F32)).astype(BF16)
        left = jnp.concatenate([table_hi, table_lo, table_hi], axis=1)
        effect = dot(left, jnp.concatenate([first, first, second], axis=1), NT) * (2.0 / SAMPLES)
        return [base[r, :, 0:BLK] - precond * effect[:, r * BLK : (r + 1) * BLK] for r in range(RC)]

    for r, value in enumerate(settle()):
        cur[r, :, 0:BLK] = value
    ext2[1, 1:5] = cur[...].astype(BF16)
    halo2 = halo(ext2, 1)
    for copy in halo2:
        copy.start()
    split(xw, spread(ext2[1, 1:5], mixer))
    acc[...] = jnp.zeros(acc.shape, F32)

    def again(g, carry):
        k = g * GROUP
        lhs = turned[pl.ds(k, GROUP)].reshape(GROUP * BLK, 128)
        product = dot(twice(lhs), xw[...], NN)
        mask = [masks(k + j) for j in range(GROUP)]
        for r in range(RC):
            lanes = slice(r * SAMPLES, (r + 1) * SAMPLES)
            total = acc[:, lanes]
            for j in range(GROUP):
                total = total + product[j * BLK : (j + 1) * BLK, lanes] * mask[j][r]
            acc[:, lanes] = total
        return carry

    lax.fori_loop(0, SLOTS // GROUP, again, 0)
    eye128 = (spot == iota((128, 128), 1)).astype(F32)
    high, low = fronts[:, 0:1], fronts[:, 64:65]
    major = jnp.floor(high * 0.25)
    minor = (high - 4.0 * major) * 32.0 + low
    onehot_lo[...] = (minor == iota((128, 128), 1).astype(F32)).astype(F32)
    major_row = jnp.sum(eye128 * major, axis=0, keepdims=True)
    onehot_hi[...] = (major_row == iota((8, 128), 0).astype(F32)).astype(F32)
    finish_halo(ext2, halo2)
    smooth(ext2)
    for r, value in enumerate(settle()):
        adj_ref[0, :, r * BLK : (r + 1) * BLK] = value[0:HARM]
        cur[r, :, 0:BLK] = value
    bw[...] = spread(cur[...].astype(BF16), mixer)[0:BLK]

    def part(g, carry):
        for j in range(8):
            k = 8 * g + j
            code = jnp.broadcast_to(codes[pl.ds(k, 1), :], (BLK, SAMPLES))
            rows = [bw[:, r * SAMPLES : (r + 1) * SAMPLES] for r in range(RC)]
            weight = jnp.where(code == 1.0, rows[0], jnp.where(code == 2.0, rows[1], jnp.where(code == 3.0, rows[2], rows[3])))
            sums[pl.ds(k, 1), :] = jnp.sum(chosen[k] * weight, axis=0, keepdims=True)
        return carry

    lax.fori_loop(0, SLOTS // 8, part, 0)
    parts = jnp.sum(sums[...], axis=1, keepdims=True) * (-sens_scale * 2.0 / SAMPLES)
    own = dot(onehot_hi[...], onehot_lo[...] * parts, NN, HIGHEST)

    def everyone(peers, me, out_of, into, send, recv):
        def copies(j):
            there = lax.rem(me + j, 8)
            going = pltpu.make_async_remote_copy(
                src_ref=out_of(there), dst_ref=into.at[me], send_sem=send.at[j], recv_sem=recv.at[me],
                device_id=peers(there), device_id_type=MESH,
            )
            coming = pltpu.make_async_remote_copy(
                src_ref=out_of(there), dst_ref=into.at[there], send_sem=send.at[j], recv_sem=recv.at[there],
                device_id=peers(there), device_id_type=MESH,
            )
            return going, coming

        pairs = [copies(j) for j in range(1, 8)]
        for going, _ in pairs:
            going.start()
        for _, coming in pairs:
            coming.wait_recv()
        total = into[0]
        for n in range(1, 8):
            total = total + into[n]
        return total, [going for going, _ in pairs]

    part_a[...] = own
    recv_a[ci] = own
    total, sent_a = everyone(lambda j: (ax, j), ci, lambda j: part_a, recv_a, a_send, a_recv)
    for n in range(8):
        part_b[n] = total[n : n + 1]
    recv_b[xy] = part_b[xy]
    total, sent_b = everyone(lambda j: (j * 8 + zz, ci), xy, lambda j: part_b.at[j], recv_b, b_send, b_recv)
    part_c[...] = total
    recv_c[zz] = total
    total, sent_c = everyone(lambda j: (xy * 8 + j, ci), zz, lambda j: part_c, recv_c, c_send, c_recv)
    sens_ref[...] = pltpu.roll(jnp.broadcast_to(total, (8, 128)), lax.rem(128 - 16 * zz, 128), 1)

    for copy in halo1 + halo2 + sent_a + sent_b + sent_c:
        copy.wait_send()

    def drain(i, carry):
        block_copy(i).wait_send()
        return carry

    lax.fori_loop(SECTIONS - WINDOW, SECTIONS, drain, 0)


def finish(adj_ref, sums_ref, adj_out, sens_out):
    adj_out[:, 0, :] = adj_ref[0]
    sens_out[...] = sums_ref[0, 0:16]


def shards(
    lam_start, rhs, state, blocks, slots, mass, precond, contact_blocks, contact_flags,
    contact_owner, contact_row, contact_front,
):
    packed = contact_blocks.reshape(CPD, 24, 3, 128).transpose(0, 2, 1, 3).reshape(CPD, LEN, 128)
    table = jnp.asarray(time_table())
    vmem = pl.BlockSpec(memory_space=pltpu.VMEM)
    smem = pl.BlockSpec(memory_space=pltpu.SMEM)
    dma = pltpu.SemaphoreType.DMA
    scratch = [
        pltpu.VMEM((8, SLOTS), jnp.int32),
        pltpu.SMEM((8, SLOTS), jnp.int32),
        pltpu.VMEM((SECTIONS, 8, 128), BF16),
        pltpu.VMEM((SECTIONS, MSG, 128), BF16),
        pltpu.VMEM((SECTIONS, MSG, 128), BF16),
        pltpu.VMEM((2, 128, 128), F32),
        pltpu.VMEM((SLOTS, BLK, 128), BF16),
        pltpu.VMEM((SLOTS, BLK, SAMPLES), F32),
        pltpu.VMEM((BLK, RC * SAMPLES), F32),
        pltpu.VMEM((SLOTS, 128), F32),
        pltpu.VMEM((SLOTS, 128), F32),
        pltpu.VMEM((SLOTS, 128), F32),
        pltpu.VMEM((8, SLOTS), F32),
        pltpu.VMEM((RC, 48, 128), F32),
        pltpu.VMEM((RC, 48, 128), F32),
        pltpu.VMEM((RC, 48, 128), F32),
        pltpu.VMEM((3, 6, 48, 128), BF16),
        pltpu.VMEM((3, 6, 48, 128), BF16),
        pltpu.VMEM((NNZ, BLK, 128), F32),
        pltpu.VMEM((RC, 48, 128), F32),
        pltpu.VMEM((256, RC * SAMPLES), BF16),
        pltpu.VMEM((256, RC * SAMPLES), BF16),
        pltpu.VMEM((2, RC * 48, RC * SAMPLES), BF16),
        pltpu.VMEM((BLK, RC * SAMPLES), F32),
        pltpu.VMEM((SLOTS, 128), F32),
        pltpu.VMEM((8, 128), F32),
        pltpu.VMEM((8, 8, 128), F32),
        pltpu.VMEM((8, 1, 128), F32),
        pltpu.VMEM((8, 1, 128), F32),
        pltpu.VMEM((1, 128), F32),
        pltpu.VMEM((8, 1, 128), F32),
        dma((1,)), dma((SECTIONS,)), dma((SECTIONS,)),
        dma((2, 8)), dma((2, 8)), dma((8,)), dma((8,)), dma((8,)), dma((8,)), dma((8,)), dma((8,)),
    ]
    adjoint, sums = pl.pallas_call(
        kernel,
        out_shape=(
            jax.ShapeDtypeStruct((1, HARM, RC * BLK), F32),
            jax.ShapeDtypeStruct((8, 128), F32),
        ),
        in_specs=[vmem, vmem, vmem, vmem, smem] + [vmem] * 8,
        out_specs=(vmem, vmem),
        scratch_shapes=scratch,
        compiler_params=pltpu.CompilerParams(
            collective_id=0, has_side_effects=True, vmem_limit_bytes=56 * 2**20
        ),
        cost_estimate=pl.CostEstimate(flops=4 * 10**9, bytes_accessed=3 * 10**6, transcendentals=0),
    )(
        lam_start, rhs, state, blocks, slots, mass, precond, packed, contact_flags,
        contact_owner.reshape(1, CPD), contact_row.reshape(1, CPD), contact_front.reshape(1, CPD), table,
    )
    adjoint, sums = pl.pallas_call(
        finish,
        out_shape=(
            jax.ShapeDtypeStruct((HARM, 1, RC * BLK), F32),
            jax.ShapeDtypeStruct((16,), F32),
        ),
        in_specs=[vmem, vmem],
        out_specs=(vmem, vmem),
    )(adjoint, sums)
    return adjoint.transpose(1, 0, 2), sums


def solution(mesh):
    in_specs = (
        P("ax", None, "circ"),
        P("ax", None, "circ"),
        P("ax", None, "circ"),
        P("ax", None, None),
        P("ax", None),
        P("ax", None),
        P("ax", None),
        P(("ax", "circ"), None),
        P(("ax", "circ"), None),
        P(("ax", "circ")),
        P(("ax", "circ")),
        P(("ax", "circ")),
    )
    out_specs = (P("ax", None, "circ"), P("ax"))
    return jax.shard_map(shards, mesh=mesh, in_specs=in_specs, out_specs=out_specs, check_vma=False)
```
